32 devices in a mesh: mask: 2 (over x), gx: 16 (over z, y, core).
Axes of the slice: x: 2, y: 2, z: 4, core: 2. Of those that a mesh axis runs over, the one named last changes fastest.
Arguments:
- e_field: float32 [3, 192, 24, 768], P(None, ('mask', 'gx')), parts along dimension 1, may hold values from -6 to 6
- h_field: float32 [3, 192, 24, 768], P(None, ('mask', 'gx')), parts along dimension 1, may hold values from -6 to 6
- polar: float32 [3, 192, 24, 768], P(None, ('mask', 'gx')), parts along dimension 1, may hold values from -6 to 6
- current: float32 [3, 192, 24, 768], P(None, ('mask', 'gx')), parts along dimension 1, may hold values from -6 to 6
- psi_h: float32 [2, 192, 6, 768], P(None, ('mask', 'gx')), parts along dimension 1, may hold values from -6 to 6
- psi_e: float32 [2, 192, 6, 768], P(None, ('mask', 'gx')), parts along dimension 1, may hold values from -6 to 6
- material: int32 [192, 24, 768], P(('mask', 'gx')), parts along dimension 0, may hold values from 0 to 3, as said below
- inv_eps_table: float32 [4], replicated, may hold values from 0.3 to 1
- decay_table: float32 [4], replicated, may hold values from 0.3 to 0.95
- drive_table: float32 [4], replicated, may hold values from 0.1 to 0.5
- strength_table: float32 [4], replicated, may hold values from 0.2 to 1
- spring_table: float32 [4], replicated, may hold values from 0.05 to 1
- orders: int32 [2, 4096], replicated, may hold values from -32 to 31
Outputs:
- e_out: float32 [3, 192, 24, 768], P(None, ('mask', 'gx')), parts along dimension 1
- h_out: float32 [3, 192, 24, 768], P(None, ('mask', 'gx')), parts along dimension 1
- polar_out: float32 [3, 192, 24, 768], P(None, ('mask', 'gx')), parts along dimension 1
- current_out: float32 [3, 192, 24, 768], P(None, ('mask', 'gx')), parts along dimension 1
- psi_h_out: float32 [2, 192, 6, 768], P(None, ('mask', 'gx')), parts along dimension 1
- psi_e_out: float32 [2, 192, 6, 768], P(None, ('mask', 'gx')), parts along dimension 1
- pupil: float32 [4, 8192], P(None, 'mask'), parts along dimension 1
The draws below stay inside these ranges and needn't reach their ends.
There are 2 independent parts, one for each index of `mask`. The reference program is written for one: setup_inputs(seed, part) draws one part's arguments, and reference() takes and returns one part's arrays. A program takes and returns all parts, laid end to end along the dimension named above; an argument that names none is the same for every part. Nothing has to cross between parts.
Inputs may be any that keep to these rules, and one draw needn't show every extreme that they name: `material`: 0 is vacuum, 1 absorber, 2 molybdenum, 3 silicon.
All inputs are finite; a program needn't handle non-finite values.
Results may differ from the reference program's by a relative error of at most 0.000082.
Values sent between devices are 32-bit elements; how exact they have to be, the bound alone decides.
A program may use at most 64 MiB of HBM per device.

```python
import math
import jax
import jax.numpy as jnp
from jax import lax

NY = 768
NZ = 24
NPML = 6
ABSORB = 6
NMAT = 4
KSPAN = 64
ORDERS = 4096
STEPS = 4
NX = 96


def draw_material(key, part):
    key_pattern, key_thick, key_rough = jax.random.split(key, 3)
    pattern = jax.random.randint(key_pattern, (NX, NY), 0, 2).astype(jnp.int32)
    thick = jax.random.randint(key_thick, (NZ,), 1, 4).astype(jnp.int32)
    bounds = jnp.cumsum(thick)
    rough = jax.random.randint(key_rough, (NX, NY), 0, 2).astype(jnp.int32)
    levels = jnp.arange(NZ + 2, dtype=jnp.int32)
    layer_table = jnp.sum((bounds[None, :] <= levels[:, None]).astype(jnp.int32), axis=1)
    rows = jnp.arange(NZ, dtype=jnp.int32)
    depth = rows - NPML - ABSORB
    shifted = jnp.clip(depth[None, :, None] + rough[:, None, :], 0, NZ + 1)
    layer = jnp.take(layer_table, shifted)
    stack = 2 + layer % 2
    top = jnp.where(rows < NPML, 0, 1)[None, :, None] * pattern[:, None, :]
    result = jnp.where((rows < NPML + ABSORB)[None, :, None], top, stack)
    return result.astype(jnp.int32)


def touch_ends(drawn, stream_key, smallest, high):
    dims = drawn.shape
    spot = [jax.random.randint(jax.random.fold_in(stream_key, axis), (), 0, dims[axis]) for axis in range(len(dims))]
    drawn = drawn.at[tuple(spot)].set(smallest)
    longest = dims.index(max(dims))
    spot[longest] = (spot[longest] + 1) % dims[longest]
    return drawn.at[tuple(spot)].set(high)


def block_levels(stream_key, shape, shards, low, high):
    factor_of = 1.0
    for axis_at, shards_of in shards:
        heights = jax.random.uniform(jax.random.fold_in(jax.random.fold_in(stream_key, 6), axis_at), (shards_of,), jnp.float32, low / len(shards), high / len(shards))
        factor_of = factor_of * jnp.repeat(jnp.exp(heights), shape[axis_at] // shards_of).reshape((-1,) + (1,) * (len(shape) - 1 - axis_at))
    return factor_of


def normal_values(rng, dims, scale, reach, shards=(), held_as=jnp.bfloat16):
    values = scale * jax.random.normal(rng, dims, jnp.float32)
    if shards:
        values = values * block_levels(rng, dims, shards, -0.22, 0.18)
    return jnp.clip(values, -reach, reach).astype(held_as)


def setup_inputs(seed: int = 0, part: int = 0) -> dict:
    streams_of = jax.random.split(jax.random.key(seed), 14)
    part_keys = jax.random.split(jax.random.fold_in(streams_of[13], part), 14)
    return {
        "e_field": normal_values(part_keys[0], (3, NX, NZ, NY), 1.0, 6.0, ((1, 16),), jnp.float32),
        "h_field": normal_values(part_keys[1], (3, NX, NZ, NY), 1.0, 6.0, ((1, 16),), jnp.float32),
        "polar": normal_values(part_keys[2], (3, NX, NZ, NY), 1.0, 6.0, ((1, 16),), jnp.float32),
        "current": normal_values(part_keys[3], (3, NX, NZ, NY), 1.0, 6.0, ((1, 16),), jnp.float32),
        "psi_h": normal_values(part_keys[4], (2, NX, NPML, NY), 1.0, 6.0, ((1, 16),), jnp.float32),
        "psi_e": normal_values(part_keys[5], (2, NX, NPML, NY), 1.0, 6.0, ((1, 16),), jnp.float32),
        "material": draw_material(jax.random.fold_in(jax.random.fold_in(streams_of[13], part), 71), part),
        "inv_eps_table": jnp.clip(jnp.exp(jax.random.uniform(streams_of[7], (NMAT,), jnp.float32, math.log(0.3), math.log(1.0))), 0.3, 1.0),
        "decay_table": jnp.clip(jax.random.uniform(streams_of[8], (NMAT,), jnp.float32, 0.3, 0.95), 0.3, 0.95),
        "drive_table": jnp.clip(jax.random.uniform(streams_of[9], (NMAT,), jnp.float32, 0.1, 0.5), 0.1, 0.5),
        "strength_table": jnp.clip(jax.random.uniform(streams_of[10], (NMAT,), jnp.float32, 0.2, 1.0), 0.2, 1.0),
        "spring_table": jnp.clip(jax.random.uniform(streams_of[11], (NMAT,), jnp.float32, 0.05, 1.0), 0.05, 1.0),
        "orders": touch_ends(jax.random.randint(streams_of[12], (2, ORDERS), 0 - KSPAN // 2, KSPAN // 2), jax.random.fold_in(streams_of[12], 1), 0 - KSPAN // 2, (KSPAN // 2) - 1).astype(jnp.int32),
    }


COURANT = 0.5
SIGMA_MAX = 0.8
PML_ALPHA = 0.05

def z_forward(field):
    after = jnp.concatenate([field[..., 1:, :], jnp.zeros_like(field[..., :1, :])], axis=-2)
    return after - field

def z_backward(field):
    before = jnp.concatenate([jnp.zeros_like(field[..., :1, :]), field[..., :-1, :]], axis=-2)
    return field - before

def y_forward(field):
    return jnp.roll(field, -1, axis=-1) - field

def y_backward(field):
    return field - jnp.roll(field, 1, axis=-1)

def pad_rows(memory, total):
    return jnp.pad(memory, ((0, 0), (0, total - memory.shape[-2]), (0, 0)))

def pml_coefficients(layers, offset):
    depth = (layers - jnp.arange(layers, dtype=jnp.float32) - offset) / layers
    sigma = SIGMA_MAX * depth ** 3
    decay = jnp.exp(-(sigma + PML_ALPHA))
    gain = sigma / (sigma + PML_ALPHA) * (decay - 1.0)
    return (decay[:, None], gain[:, None])

def lookup(material, table):
    total = jnp.zeros(material.shape, table.dtype)
    for index in range(table.shape[0]):
        total = total + jnp.where(material == index, table[index], 0.0)
    return total

def h_update(e_x, e_y, e_z, ey_ahead, ez_ahead, h_x, h_y, h_z, psi_hx, psi_hy, decay, gain):
    layers = psi_hx.shape[-2]
    depth_cells = e_x.shape[-2]
    dey_dz = z_forward(e_y)
    dex_dz = z_forward(e_x)
    psi_hx_new = decay * psi_hx + gain * dey_dz[:, :layers]
    psi_hy_new = decay * psi_hy + gain * dex_dz[:, :layers]
    hx_new = h_x - COURANT * (y_forward(e_z) - dey_dz - pad_rows(psi_hx_new, depth_cells))
    hy_new = h_y - COURANT * (dex_dz + pad_rows(psi_hy_new, depth_cells) - (ez_ahead - e_z))
    hz_new = h_z - COURANT * (ey_ahead - e_y - y_forward(e_x))
    return (hx_new, hy_new, hz_new, psi_hx_new, psi_hy_new)

def e_update(hx_new, hy_new, hz_new, hy_behind, hz_behind, psi_ex, psi_ey, decay, gain, e_field, polar, current, coefs):
    inv_eps, decay_j, drive_j, strength, spring = coefs
    layers = psi_ex.shape[-2]
    depth_cells = hx_new.shape[-2]
    dhy_dz = z_backward(hy_new)
    dhx_dz = z_backward(hx_new)
    psi_ex_new = decay * psi_ex + gain * dhy_dz[:, :layers]
    psi_ey_new = decay * psi_ey + gain * dhx_dz[:, :layers]
    curl_x = y_backward(hz_new) - (dhy_dz + pad_rows(psi_ex_new, depth_cells))
    curl_y = dhx_dz + pad_rows(psi_ey_new, depth_cells) - (hz_new - hz_behind)
    curl_z = hy_new - hy_behind - y_backward(hx_new)
    curl = jnp.stack([curl_x, curl_y, curl_z])
    current_new = decay_j * current + drive_j * (strength * e_field - spring * polar)
    polar_new = polar + current_new
    e_new = e_field + inv_eps * (COURANT * curl - current_new)
    return (e_new, polar_new, current_new, psi_ex_new, psi_ey_new)

def y_table(cells, span):
    rows = jnp.arange(cells, dtype=jnp.int32)
    waves = jnp.arange(span, dtype=jnp.int32) - span // 2
    phase = (rows[:, None] * waves[None, :] % cells).astype(jnp.float32) * (2.0 * math.pi / cells)
    return jnp.concatenate([jnp.cos(phase), jnp.sin(phase)], axis=1)

def x_table(rows, cells, span):
    waves = jnp.arange(span, dtype=jnp.int32) - span // 2
    phase = (rows[:, None] * waves[None, :] % cells).astype(jnp.float32) * (2.0 * math.pi / cells)
    return (jnp.cos(phase), jnp.sin(phase))

def local_spectrum(plane, rows, cells_x, span):
    comps, planes, cells_y = plane.shape
    highest = lax.Precision.HIGHEST
    table = y_table(cells_y, span)
    mixed = jnp.dot(plane.reshape(comps * planes, cells_y), table, precision=highest, preferred_element_type=jnp.float32)
    mixed = mixed.reshape(comps, planes, 2, span)
    real_y = mixed[:, :, 0]
    imag_y = -mixed[:, :, 1]
    cos_x, sin_x = x_table(rows, cells_x, span)
    real = jnp.einsum('cxk,xj->cjk', real_y, cos_x, precision=highest) + jnp.einsum('cxk,xj->cjk', imag_y, sin_x, precision=highest)
    imag = jnp.einsum('cxk,xj->cjk', imag_y, cos_x, precision=highest) - jnp.einsum('cxk,xj->cjk', real_y, sin_x, precision=highest)
    return jnp.stack([real, imag], axis=1)

def pick_orders(spectrum, orders, cells_total):
    span = spectrum.shape[-1]
    flat = spectrum.reshape(4, span * span) / math.sqrt(cells_total)
    index = ((orders[0] + span // 2) * span + (orders[1] + span // 2)).astype(jnp.int32)
    return jnp.take(flat, index, axis=1)

def reference(e_field, h_field, polar, current, psi_h, psi_e, material, inv_eps_table, decay_table, drive_table, strength_table, spring_table, orders):
    coefs = tuple((lookup(material, table) for table in (inv_eps_table, decay_table, drive_table, strength_table, spring_table)))
    decay_h, gain_h = pml_coefficients(NPML, 0.5)
    decay_e, gain_e = pml_coefficients(NPML, 0.0)
    for step in range(STEPS):
        e_x, e_y, e_z = (e_field[0], e_field[1], e_field[2])
        hx_new, hy_new, hz_new, psi_hx, psi_hy = h_update(e_x, e_y, e_z, jnp.roll(e_y, -1, 0), jnp.roll(e_z, -1, 0), h_field[0], h_field[1], h_field[2], psi_h[0], psi_h[1], decay_h, gain_h)
        h_field = jnp.stack([hx_new, hy_new, hz_new])
        psi_h = jnp.stack([psi_hx, psi_hy])
        e_field, polar, current, psi_ex, psi_ey = e_update(hx_new, hy_new, hz_new, jnp.roll(hy_new, 1, 0), jnp.roll(hz_new, 1, 0), psi_e[0], psi_e[1], decay_e, gain_e, e_field, polar, current, coefs)
        psi_e = jnp.stack([psi_ex, psi_ey])
    rows = jnp.arange(NX, dtype=jnp.int32)
    spectrum = local_spectrum(e_field[0:2, :, NPML, :], rows, NX, KSPAN)
    pupil = pick_orders(spectrum, orders, NX * NY)
    return (e_field, h_field, polar, current, psi_h, psi_e, pupil)
```

```python
import functools
import math

import jax
import jax.numpy as jnp
import numpy as np
from jax import lax
from jax.experimental import pallas as pl
from jax.experimental.pallas import tpu as pltpu
from jax.sharding import PartitionSpec as P

KSPAN = 64
STEPS = 4
COURANT = 0.5
SIGMA_MAX = 0.8
PML_ALPHA = 0.05
ROWS = 8
LANES = 128


def profile_table(layers):
    out = []
    for offset in (0.5, 0.0):
        depth = (layers - np.arange(layers, dtype=np.float64) - offset) / layers
        sigma = SIGMA_MAX * depth**3
        decay = np.exp(-(sigma + PML_ALPHA))
        gain = sigma / (sigma + PML_ALPHA) * (decay - 1.0)
        for values in (decay, gain):
            column = np.zeros((ROWS, 1))
            column[:layers, 0] = values
            out.append(np.broadcast_to(column, (ROWS, LANES)))
    return np.stack(out).astype(np.float32)


def wave_table(cells, span):
    rows = np.arange(cells, dtype=np.int64)
    waves = np.arange(span, dtype=np.int64) - span // 2
    phase = (rows[:, None] * waves[None, :] % cells) * (2.0 * math.pi / cells)
    return np.concatenate([np.cos(phase), np.sin(phase)], axis=1)


def x_matrix(count, planes, rows, span):
    waves = wave_table(count * planes, span).T.reshape(2 * span, count, planes)
    out = np.zeros((2, 2 * span, count, rows))
    for comp in range(2):
        out[comp, :, :, comp * planes : (comp + 1) * planes] = waves
    return out.reshape(4 * span, count * rows).astype(np.float32)


def kernel(
    count,
    layers,
    e_in,
    h_in,
    p_in,
    c_in,
    psi_h_in,
    psi_e_in,
    mat_in,
    ytab_in,
    xmat_in,
    inv_eps_table,
    decay_table,
    drive_table,
    strength_table,
    spring_table,
    prof,
    orders,
    e,
    h,
    pol,
    cur,
    psi_h_out,
    psi_e_out,
    pupil,
    mat,
    coefs,
    psi_h,
    psi_e,
    ahead,
    behind,
    halo,
    halo_psi,
    ytab,
    xmat,
    line,
    gathered,
    local_sem,
    left_send,
    left_recv,
    right_send,
    right_recv,
    first_send,
    first_recv,
    all_send,
    all_recv,
):
    planes, depth, cells = mat.shape
    tiles = depth // ROWS
    me = lax.axis_index("gx")
    right, left = lax.rem(me + 1, count), lax.rem(me + count - 1, count)

    barrier = pltpu.get_barrier_semaphore()

    def greet(k, carry):
        pl.semaphore_signal(
            barrier,
            inc=1,
            device_id={"gx": lax.rem(me + k, count)},
            device_id_type=pl.DeviceIdType.MESH,
        )
        return carry

    lax.fori_loop(1, count, greet, 0)
    loads = [
        pltpu.make_async_copy(source, target, local_sem.at[index])
        for index, (source, target) in enumerate(
            [
                (e_in, e),
                (h_in, h),
                (mat_in, mat),
                (c_in, cur),
                (p_in, pol),
                (ytab_in, ytab),
                (xmat_in, xmat),
            ]
        )
    ]
    for load in loads:
        load.start()

    row = lax.broadcasted_iota(jnp.int32, (ROWS, cells), 0)
    first_row = row == 0
    last_row = row == ROWS - 1

    def wide(index):
        return jnp.concatenate([prof[index]] * (cells // LANES), axis=1)

    def tile(ref, t):
        return ref[t * ROWS : (t + 1) * ROWS, :]

    def z_next(ref, t):
        moved = pltpu.roll(tile(ref, t), ROWS - 1, 0)
        if t == tiles - 1:
            return jnp.where(last_row, 0.0, moved)
        return jnp.where(last_row, ref[(t + 1) * ROWS : (t + 1) * ROWS + 1, :], moved)

    def z_prev(ref, t):
        moved = pltpu.roll(tile(ref, t), 1, 0)
        if t == 0:
            return jnp.where(first_row, 0.0, moved)
        return jnp.where(first_row, ref[t * ROWS - 1 : t * ROWS, :], moved)

    def y_next(value):
        return pltpu.roll(value, cells - 1, 1)

    def y_prev(value):
        return pltpu.roll(value, 1, 1)

    def h_plane(ex, ey, ez, ey2, ez2, hx, hy, hz, psx, psy):
        for t in range(tiles):
            at = slice(t * ROWS, (t + 1) * ROWS)
            x, y, z = tile(ex, t), tile(ey, t), tile(ez, t)
            dex = z_next(ex, t) - x
            if t == 0:
                mem = wide(0) * psy[...] + wide(1) * dex
                psy[...] = mem
                dex = dex + mem
            if hx is not None:
                dey = z_next(ey, t) - y
                if t == 0:
                    mem = wide(0) * psx[...] + wide(1) * dey
                    psx[...] = mem
                    dey = dey + mem
                hx[at, :] = tile(hx, t) - COURANT * (y_next(z) - z - dey)
            hy[at, :] = tile(hy, t) - COURANT * (dex - (tile(ez2, t) - z))
            hz[at, :] = tile(hz, t) - COURANT * (tile(ey2, t) - y - (y_next(x) - x))

    def e_plane(p, hy_b, hz_b):
        hx, hy, hz = h.at[0, p], h.at[1, p], h.at[2, p]
        for t in range(tiles):
            at = slice(t * ROWS, (t + 1) * ROWS)
            x, y, z = tile(hx, t), tile(hy, t), tile(hz, t)
            dhy = y - z_prev(hy, t)
            dhx = x - z_prev(hx, t)
            if t == 0:
                mem = wide(2) * psi_e[0, p] + wide(3) * dhy
                psi_e[0, p] = mem
                dhy = dhy + mem
                mem = wide(2) * psi_e[1, p] + wide(3) * dhx
                psi_e[1, p] = mem
                dhx = dhx + mem
            curl = (
                z - y_prev(z) - dhy,
                dhx - (z - tile(hz_b, t)),
                y - tile(hy_b, t) - (x - y_prev(x)),
            )
            inv_eps = coefs[0, p, at, :]
            decay = coefs[1, p, at, :]
            pull = coefs[2, p, at, :]
            hold = coefs[3, p, at, :]
            for c in range(3):
                field = e[c, p, at, :]
                polar = pol[c, p, at, :]
                current = decay * cur[c, p, at, :] + (pull * field - hold * polar)
                cur[c, p, at, :] = current
                pol[c, p, at, :] = polar + current
                e[c, p, at, :] = field + inv_eps * (COURANT * curl[c] - current)

    def to_left(step):
        return pltpu.make_async_remote_copy(
            src_ref=e.at[1:3, 0],
            dst_ref=ahead.at[step],
            send_sem=left_send.at[step],
            recv_sem=left_recv.at[step],
            device_id={"gx": left},
            device_id_type=pl.DeviceIdType.MESH,
        )

    def to_right(step):
        return pltpu.make_async_remote_copy(
            src_ref=e.at[:, planes - 1],
            dst_ref=behind.at[step],
            send_sem=right_send.at[step],
            recv_sem=right_recv.at[step],
            device_id={"gx": right},
            device_id_type=pl.DeviceIdType.MESH,
        )

    firsts = [
        pltpu.make_async_remote_copy(
            src_ref=source,
            dst_ref=target,
            send_sem=first_send.at[index],
            recv_sem=first_recv.at[index],
            device_id={"gx": right},
            device_id_type=pl.DeviceIdType.MESH,
        )
        for index, (source, target) in enumerate(
            [(h.at[1:3, planes - 1], halo), (psi_h.at[1, planes - 1], halo_psi)]
        )
    ]

    def fill_psi(p, carry):
        for source, target in ((psi_h_in, psi_h), (psi_e_in, psi_e)):
            for c in range(2):
                target[c, p] = jnp.zeros((ROWS, cells), jnp.float32)
                for z in range(layers):
                    target[c, p, z : z + 1, :] = source[p, z, c : c + 1, :]
        return carry

    lax.fori_loop(0, planes, fill_psi, 0)
    loads[0].wait()
    loads[1].wait()
    pl.semaphore_wait(barrier, count - 1)
    to_left(0).start()
    to_right(0).start()
    for first in firsts:
        first.start()

    materials = inv_eps_table.shape[0]
    pulls = [drive_table[i] * strength_table[i] for i in range(materials)]
    holds = [drive_table[i] * spring_table[i] for i in range(materials)]
    tables = (
        [inv_eps_table[i] for i in range(materials)],
        [decay_table[i] for i in range(materials)],
        pulls,
        holds,
    )
    loads[2].wait()

    def fill_coefs(p, carry):
        for t in range(tiles):
            at = slice(t * ROWS, (t + 1) * ROWS)
            m = mat[p, at, :]
            same = [m == i for i in range(materials)]
            for index, table in enumerate(tables):
                value = jnp.zeros((ROWS, cells), jnp.float32)
                for i in range(materials):
                    value = jnp.where(same[i], table[i], value)
                coefs[index, p, at, :] = value
        return carry

    lax.fori_loop(0, planes, fill_coefs, 0)

    def h_own(p, ey2, ez2):
        h_plane(
            e.at[0, p], e.at[1, p], e.at[2, p], ey2, ez2,
            h.at[0, p], h.at[1, p], h.at[2, p], psi_h.at[0, p], psi_h.at[1, p],
        )

    def run_step(step, carry):
        def h_inner(p, c):
            h_own(p, e.at[1, p + 1], e.at[2, p + 1])
            return c

        lax.fori_loop(0, planes - 1, h_inner, 0)

        @pl.when(step == 0)
        def _():
            for first in firsts:
                first.wait()
            for load in loads[3:5]:
                load.wait()

        to_left(step).wait()
        h_own(planes - 1, ahead.at[step, 0], ahead.at[step, 1])
        to_right(step).wait()
        h_plane(
            behind.at[step, 0], behind.at[step, 1], behind.at[step, 2],
            e.at[1, 0], e.at[2, 0], None, halo.at[0], halo.at[1], None, halo_psi,
        )
        e_plane(0, halo.at[0], halo.at[1])
        e_plane(planes - 1, h.at[1, planes - 2], h.at[2, planes - 2])

        @pl.when(step < STEPS - 1)
        def _():
            to_left(step + 1).start()
            to_right(step + 1).start()

        def e_inner(p, c):
            e_plane(p, h.at[1, p - 1], h.at[2, p - 1])
            return c

        lax.fori_loop(1, planes - 1, e_inner, 0)
        return carry

    lax.fori_loop(0, STEPS, run_step, 0)

    line[...] = jnp.zeros(line.shape, jnp.float32)
    for c in range(2):
        for p in range(planes):
            line[c * planes + p : c * planes + p + 1, :] = e[c, p, layers : layers + 1, :]
    loads[5].wait()
    gathered[me] = jnp.dot(
        line[...],
        ytab[...],
        precision=lax.Precision.HIGHEST,
        preferred_element_type=jnp.float32,
    )

    def share(k):
        return pltpu.make_async_remote_copy(
            src_ref=gathered.at[me],
            dst_ref=gathered.at[me],
            send_sem=all_send.at[k],
            recv_sem=all_recv.at[me],
            device_id={"gx": lax.rem(me + k, count)},
            device_id_type=pl.DeviceIdType.MESH,
        )

    def start_share(k, carry):
        share(k).start()
        return carry

    lax.fori_loop(1, count, start_share, 0)

    def drain_psi(p, carry):
        for source, target in ((psi_h, psi_h_out), (psi_e, psi_e_out)):
            for c in range(2):
                for z in range(layers):
                    target[p, z, c : c + 1, :] = source[c, p, z : z + 1, :]
        return carry

    lax.fori_loop(0, planes, drain_psi, 0)
    loads[6].wait()

    def end_share(k, carry):
        other = lax.rem(me + k, count)
        pltpu.make_async_remote_copy(
            src_ref=gathered.at[other],
            dst_ref=gathered.at[other],
            send_sem=all_send.at[k],
            recv_sem=all_recv.at[other],
            device_id={"gx": other},
            device_id_type=pl.DeviceIdType.MESH,
        ).wait_recv()
        return carry

    def end_send(k, carry):
        share(k).wait_send()
        return carry

    lax.fori_loop(1, count, end_share, 0)
    lax.fori_loop(1, count, end_send, 0)

    span = KSPAN
    waves = jnp.dot(
        xmat[...],
        gathered[...].reshape(count * line.shape[0], 2 * span),
        precision=lax.Precision.HIGHEST,
        preferred_element_type=jnp.float32,
    )
    scale = 1.0 / math.sqrt(count * planes * cells)
    flats = []
    for c in range(2):
        cosine = waves[2 * c * span : (2 * c + 1) * span]
        sine = waves[(2 * c + 1) * span : (2 * c + 2) * span]
        flats.append(cosine - pltpu.roll(sine, span, 1))
        flats.append(-(pltpu.roll(cosine, span, 1) + sine))
    flat = jnp.concatenate(flats, axis=0)[:, :span] * scale
    pieces = []
    for _ in range(3):
        piece = flat.astype(jnp.bfloat16)
        pieces.append(piece)
        flat = flat - piece.astype(jnp.float32)
    left_side = jnp.concatenate(pieces, axis=1)

    chunk = 512
    total = orders.shape[1]
    index = lax.broadcasted_iota(jnp.int32, (span, chunk), 0) - span // 2
    for start in range(0, total, chunk):
        at = slice(start, start + chunk)
        kx = index == orders[0:1, at]
        ky = jnp.where(index == orders[1:2, at], 1.0, 0.0).astype(jnp.bfloat16)
        picked = jnp.dot(
            left_side,
            jnp.concatenate([ky] * 3, axis=0),
            preferred_element_type=jnp.float32,
        )
        for r in range(4):
            pupil[r : r + 1, at] = jnp.sum(
                jnp.where(kx, picked[r * span : (r + 1) * span], 0.0), axis=0, keepdims=True
            )


def shards(
    e_field,
    h_field,
    polar,
    current,
    psi_h,
    psi_e,
    material,
    inv_eps_table,
    decay_table,
    drive_table,
    strength_table,
    spring_table,
    orders,
):
    count = lax.axis_size("gx")
    planes, depth, cells = material.shape
    layers = psi_h.shape[2]
    f32 = jnp.float32
    rows = -(-2 * planes // ROWS) * ROWS
    prof = jnp.asarray(profile_table(layers))
    ytab = jnp.asarray(wave_table(cells, KSPAN).astype(np.float32))
    xmat = jnp.asarray(x_matrix(count, planes, rows, KSPAN))
    hbm = pl.BlockSpec(memory_space=pltpu.MemorySpace.HBM)
    vmem = pl.BlockSpec(memory_space=pltpu.MemorySpace.VMEM)
    smem = pl.BlockSpec(memory_space=pltpu.MemorySpace.SMEM)
    dma = pltpu.SemaphoreType.DMA
    turned = (planes, layers, 2, cells)
    outs = pl.pallas_call(
        functools.partial(kernel, count, layers),
        out_shape=[jax.ShapeDtypeStruct(e_field.shape, f32)] * 4
        + [jax.ShapeDtypeStruct(turned, f32)] * 2
        + [jax.ShapeDtypeStruct((4, orders.shape[1]), f32)],
        in_specs=[hbm] * 4 + [vmem] * 2 + [hbm] * 3 + [smem] * 5 + [vmem] * 2,
        out_specs=[vmem] * 7,
        scratch_shapes=[
            pltpu.VMEM(material.shape, jnp.int32),
            pltpu.VMEM((4,) + material.shape, f32),
            pltpu.VMEM((2, planes, ROWS, cells), f32),
            pltpu.VMEM((2, planes, ROWS, cells), f32),
            pltpu.VMEM((STEPS, 2, depth, cells), f32),
            pltpu.VMEM((STEPS, 3, depth, cells), f32),
            pltpu.VMEM((2, depth, cells), f32),
            pltpu.VMEM((ROWS, cells), f32),
            pltpu.VMEM(ytab.shape, f32),
            pltpu.VMEM(xmat.shape, f32),
            pltpu.VMEM((rows, cells), f32),
            pltpu.VMEM((count, rows, 2 * KSPAN), f32),
            dma((7,)),
            dma((STEPS,)),
            dma((STEPS,)),
            dma((STEPS,)),
            dma((STEPS,)),
            dma((2,)),
            dma((2,)),
            dma((count,)),
            dma((count,)),
        ],
        compiler_params=pltpu.CompilerParams(
            collective_id=0, has_side_effects=True, vmem_limit_bytes=40 * 1024 * 1024
        ),
    )(
        e_field,
        h_field,
        polar,
        current,
        jnp.transpose(psi_h, (1, 2, 0, 3)),
        jnp.transpose(psi_e, (1, 2, 0, 3)),
        material,
        ytab,
        xmat,
        inv_eps_table,
        decay_table,
        drive_table,
        strength_table,
        spring_table,
        prof,
        orders,
    )
    psi_h_out = jnp.transpose(outs[4], (2, 0, 1, 3))
    psi_e_out = jnp.transpose(outs[5], (2, 0, 1, 3))
    return (outs[0], outs[1], outs[2], outs[3], psi_h_out, psi_e_out, outs[6])


def solution(mesh):
    field = P(None, ("mask", "gx"), None, None)
    in_specs = (field,) * 6 + (P(("mask", "gx"), None, None),) + (P(),) * 6
    out_specs = (field,) * 6 + (P(None, "mask"),)
    return jax.shard_map(shards, mesh=mesh, in_specs=in_specs, out_specs=out_specs, check_vma=False)
```

```python
import functools
import math

import jax
import jax.numpy as jnp
import numpy as np
from jax import lax
from jax.experimental import pallas as pl
from jax.experimental.pallas import tpu as pltpu
from jax.sharding import PartitionSpec as P

KSPAN = 64
STEPS = 4
COURANT = 0.5
SIGMA_MAX = 0.8
PML_ALPHA = 0.05
ROWS = 8
LANES = 128


def profile_values(layers):
    out = []
    for offset in (0.5, 0.0):
        depth = (layers - np.arange(layers, dtype=np.float64) - offset) / layers
        sigma = SIGMA_MAX * depth**3
        decay = np.exp(-(sigma + PML_ALPHA))
        gain = sigma / (sigma + PML_ALPHA) * (decay - 1.0)
        out += [decay, gain]
    return out


def wave_table(cells, span):
    rows = np.arange(cells, dtype=np.int64)
    waves = np.arange(span, dtype=np.int64) - span // 2
    phase = (rows[:, None] * waves[None, :] % cells) * (2.0 * math.pi / cells)
    return np.concatenate([np.cos(phase), np.sin(phase)], axis=1)


def x_matrix(count, planes, rows, span):
    waves = wave_table(count * planes, span).T.reshape(2 * span, count, planes)
    out = np.zeros((2, 2 * span, count, rows))
    for comp in range(2):
        out[comp, :, :, comp * planes : (comp + 1) * planes] = waves
    return out.reshape(4 * span, count * rows).astype(np.float32)


def step_kernel(
    count,
    layers,
    e_in,
    h_in,
    p_in,
    c_in,
    psi_h_in,
    psi_e_in,
    mat_in,
    ytab_in,
    inv_eps_table,
    decay_table,
    drive_table,
    strength_table,
    spring_table,
    e_out,
    h_out,
    p_out,
    c_out,
    psi_h_out,
    psi_e_out,
    gathered_out,
    e,
    h,
    pol,
    cur,
    raw_h,
    raw_e,
    mat,
    prof,
    coefs,
    psi_h,
    psi_e,
    ahead,
    behind,
    ytab,
    line,
    gathered,
    load_sem,
    store_sem,
    left_send,
    left_recv,
    right_send,
    right_recv,
    all_send,
    all_recv,
):
    planes, depth, cells = mat.shape
    tiles = depth // ROWS
    last = planes - 1
    me = lax.axis_index("gx")
    right, left = lax.rem(me + 1, count), lax.rem(me + count - 1, count)

    loads = [
        pltpu.make_async_copy(source, target, load_sem.at[index])
        for index, (source, target) in enumerate(
            [
                (e_in, e),
                (h_in, h),
                (psi_h_in, raw_h),
                (mat_in, mat),
                (c_in, cur),
                (p_in, pol),
                (psi_e_in, raw_e),
                (ytab_in, ytab),
            ]
        )
    ]
    for load in loads:
        load.start()
    stores = [
        pltpu.make_async_copy(source, target, store_sem.at[index])
        for index, (source, target) in enumerate(
            [
                (h, h_out),
                (e, e_out),
                (cur, c_out),
                (pol, p_out),
                (raw_h, psi_h_out),
                (raw_e, psi_e_out),
                (gathered, gathered_out),
            ]
        )
    ]

    barrier = pltpu.get_barrier_semaphore()

    def greet(k, carry):
        pl.semaphore_signal(
            barrier,
            inc=1,
            device_id={"gx": lax.rem(me + k, count)},
            device_id_type=pl.DeviceIdType.MESH,
        )
        return carry

    lax.fori_loop(1, count, greet, 0)

    level = lax.broadcasted_iota(jnp.int32, (ROWS, LANES), 0)
    for index, values in enumerate(profile_values(layers)):
        total = jnp.zeros((ROWS, LANES), jnp.float32)
        for z in range(layers):
            total = jnp.where(level == z, float(values[z]), total)
        prof[index] = total

    row = lax.broadcasted_iota(jnp.int32, (ROWS, cells), 0)
    first_row = row == 0
    last_row = row == ROWS - 1

    def wide(index):
        return jnp.concatenate([prof[index]] * (cells // LANES), axis=1)

    def rows_of(t):
        return slice(t * ROWS, (t + 1) * ROWS)

    def tile(ref, t):
        return ref[rows_of(t), :]

    def z_next(ref, t):
        moved = pltpu.roll(tile(ref, t), ROWS - 1, 0)
        if t == tiles - 1:
            return jnp.where(last_row, 0.0, moved)
        return jnp.where(last_row, ref[(t + 1) * ROWS : (t + 1) * ROWS + 1, :], moved)

    def z_prev(ref, t):
        moved = pltpu.roll(tile(ref, t), 1, 0)
        if t == 0:
            return jnp.where(first_row, 0.0, moved)
        return jnp.where(first_row, ref[t * ROWS - 1 : t * ROWS, :], moved)

    def y_next(value):
        return pltpu.roll(value, cells - 1, 1)

    def y_prev(value):
        return pltpu.roll(value, 1, 1)

    def h_tile(p, t, whole):
        at = rows_of(t)
        ex, ey = e.at[0, p], e.at[1, p]
        x, y, z = tile(ex, t), tile(ey, t), e[2, p, at, :]
        dex = z_next(ex, t) - x
        dey = z_next(ey, t) - y
        if t == 0:
            mem = wide(0) * psi_h[1, p] + wide(1) * dex
            psi_h[1, p] = mem
            dex = dex + mem
            mem = wide(0) * psi_h[0, p] + wide(1) * dey
            psi_h[0, p] = mem
            dey = dey + mem
        h[0, p, at, :] = h[0, p, at, :] - COURANT * (y_next(z) - z - dey)
        part_y = dex + z
        part_z = x - y - y_next(x)
        if whole:
            part_y = part_y - e[2, p + 1, at, :]
            part_z = part_z + e[1, p + 1, at, :]
        h[1, p, at, :] = h[1, p, at, :] - COURANT * part_y
        h[2, p, at, :] = h[2, p, at, :] - COURANT * part_z

    def e_tile(p, t, hy_b, hz_b):
        at = rows_of(t)
        hx, hy = h.at[0, p], h.at[1, p]
        x, y, z = tile(hx, t), tile(hy, t), h[2, p, at, :]
        dhy = y - z_prev(hy, t)
        dhx = x - z_prev(hx, t)
        if t == 0:
            mem = wide(2) * psi_e[0, p] + wide(3) * dhy
            psi_e[0, p] = mem
            dhy = dhy + mem
            mem = wide(2) * psi_e[1, p] + wide(3) * dhx
            psi_e[1, p] = mem
            dhx = dhx + mem
        curl = (
            z - y_prev(z) - dhy,
            dhx - (z - hz_b),
            y - hy_b - (x - y_prev(x)),
        )
        inv_eps = coefs[0, p, at, :]
        decay = coefs[1, p, at, :]
        pull = coefs[2, p, at, :]
        hold = coefs[3, p, at, :]
        for c in range(3):
            field = e[c, p, at, :]
            polar = pol[c, p, at, :]
            current = decay * cur[c, p, at, :] + (pull * field - hold * polar)
            cur[c, p, at, :] = current
            pol[c, p, at, :] = polar + current
            e[c, p, at, :] = field + inv_eps * (COURANT * curl[c] - current)

    def e_own(p, t):
        e_tile(p, t, h[1, p - 1, rows_of(t), :], h[2, p - 1, rows_of(t), :])

    def to_left(step, t):
        return pltpu.make_async_remote_copy(
            src_ref=e.at[1:3, 0, rows_of(t)],
            dst_ref=ahead.at[step, :, rows_of(t)],
            send_sem=left_send.at[step, t],
            recv_sem=left_recv.at[step, t],
            device_id={"gx": left},
            device_id_type=pl.DeviceIdType.MESH,
        )

    def to_right(step, t):
        return pltpu.make_async_remote_copy(
            src_ref=h.at[1:3, last, rows_of(t)],
            dst_ref=behind.at[step, :, rows_of(t)],
            send_sem=right_send.at[step, t],
            recv_sem=right_recv.at[step, t],
            device_id={"gx": right},
            device_id_type=pl.DeviceIdType.MESH,
        )

    def fill_psi(source, target):
        def fill(p, carry):
            for c in range(2):
                target[c, p] = jnp.zeros((ROWS, cells), jnp.float32)
                for z in range(layers):
                    target[c, p, z : z + 1, :] = source[p, z, c : c + 1, :]
            return carry

        lax.fori_loop(0, planes, fill, 0)

    def drain_psi(source, target):
        def drain(p, carry):
            for c in range(2):
                for z in range(layers):
                    target[p, z, c : c + 1, :] = source[c, p, z : z + 1, :]
            return carry

        lax.fori_loop(0, planes, drain, 0)

    for load in loads[:3]:
        load.wait()
    fill_psi(raw_h, psi_h)
    h_tile(last, 0, False)
    pl.semaphore_wait(barrier, count - 1)
    for t in range(tiles):
        to_left(0, t).start()
        if t > 0:
            h_tile(last, t, False)
        to_right(0, t).start()

    materials = inv_eps_table.shape[0]
    tables = (
        [inv_eps_table[i] for i in range(materials)],
        [decay_table[i] for i in range(materials)],
        [drive_table[i] * strength_table[i] for i in range(materials)],
        [drive_table[i] * spring_table[i] for i in range(materials)],
    )
    loads[3].wait()

    def fill_coefs(p, carry):
        for t in range(tiles):
            m = mat[p, rows_of(t), :]
            same = [m == i for i in range(materials)]
            for index, table in enumerate(tables):
                value = jnp.zeros((ROWS, cells), jnp.float32)
                for i in range(materials):
                    value = jnp.where(same[i], table[i], value)
                coefs[index, p, rows_of(t), :] = value
        return carry

    lax.fori_loop(0, planes, fill_coefs, 0)
    for load in loads[4:]:
        load.wait()
    fill_psi(raw_e, psi_e)

    def run_step(step, carry):
        def h_inner(p, c):
            for t in range(tiles):
                h_tile(p, t, True)
            return c

        lax.fori_loop(0, last, h_inner, 0)
        more = step < STEPS - 1

        def next_right(t):
            h_tile(last, t, False)
            to_right(step + 1, t).start()

        for t in range(tiles):
            at = rows_of(t)
            to_left(step, t).wait()
            to_right(step, t).wait()
            h[1, last, at, :] = h[1, last, at, :] + COURANT * ahead[step, 1, at, :]
            h[2, last, at, :] = h[2, last, at, :] - COURANT * ahead[step, 0, at, :]
            hy_b = behind[step, 0, at, :] + COURANT * e[2, 0, at, :]
            hz_b = behind[step, 1, at, :] - COURANT * e[1, 0, at, :]
            e_tile(0, t, hy_b, hz_b)

            @pl.when(more)
            def _():
                to_left(step + 1, t).start()

            e_own(last, t)

            @pl.when(more)
            def _():
                if t > 0:
                    next_right(t - 1)
                if t == tiles - 1:
                    next_right(t)

        @pl.when(jnp.logical_not(more))
        def _():
            stores[0].start()

        def e_inner(p, c):
            for t in range(tiles):
                e_own(p, t)
            return c

        lax.fori_loop(1, last, e_inner, 0)
        return carry

    lax.fori_loop(0, STEPS, run_step, 0)

    line[...] = jnp.zeros(line.shape, jnp.float32)
    for c in range(2):
        for p in range(planes):
            line[c * planes + p : c * planes + p + 1, :] = e[c, p, layers : layers + 1, :]
    gathered[me] = jnp.dot(
        line[...],
        ytab[...],
        precision=lax.Precision.HIGHEST,
        preferred_element_type=jnp.float32,
    )

    def share(k):
        return pltpu.make_async_remote_copy(
            src_ref=gathered.at[me],
            dst_ref=gathered.at[me],
            send_sem=all_send.at[k],
            recv_sem=all_recv.at[me],
            device_id={"gx": lax.rem(me + k, count)},
            device_id_type=pl.DeviceIdType.MESH,
        )

    def start_share(k, carry):
        share(k).start()
        return carry

    lax.fori_loop(1, count, start_share, 0)
    for store in stores[1:4]:
        store.start()
    drain_psi(psi_h, raw_h)
    stores[4].start()
    drain_psi(psi_e, raw_e)
    stores[5].start()

    def end_share(k, carry):
        other = lax.rem(me + k, count)
        pltpu.make_async_remote_copy(
            src_ref=gathered.at[other],
            dst_ref=gathered.at[other],
            send_sem=all_send.at[k],
            recv_sem=all_recv.at[other],
            device_id={"gx": other},
            device_id_type=pl.DeviceIdType.MESH,
        ).wait_recv()
        return carry

    def end_send(k, carry):
        share(k).wait_send()
        return carry

    lax.fori_loop(1, count, end_share, 0)
    lax.fori_loop(1, count, end_send, 0)
    stores[6].start()
    for store in stores:
        store.wait()


def result_kernel(norm, *refs):
    ins, refs = refs[:6], refs[6:]
    (gathered_in, xmat_in, orders), refs = refs[:3], refs[3:]
    outs, pupil, refs = refs[:6], refs[6], refs[7:]
    held, (gathered, xmat, in_sem, out_sem, table_sem) = refs[:6], refs[6:]

    tables = [
        pltpu.make_async_copy(gathered_in, gathered, table_sem.at[0]),
        pltpu.make_async_copy(xmat_in, xmat, table_sem.at[1]),
    ]
    for table in tables:
        table.start()
    loads, stores = [], []
    for index in range(6):
        for c in range(held[index].shape[0]):
            sem = len(loads)
            loads.append(
                pltpu.make_async_copy(ins[index].at[c], held[index].at[c], in_sem.at[sem])
            )
            stores.append(
                pltpu.make_async_copy(held[index].at[c], outs[index].at[c], out_sem.at[sem])
            )
    for load in loads:
        load.start()
    for table in tables:
        table.wait()

    span = KSPAN
    waves = jnp.dot(
        xmat[...],
        gathered[...].reshape(gathered.shape[0] * gathered.shape[1], 2 * span),
        precision=lax.Precision.HIGHEST,
        preferred_element_type=jnp.float32,
    )
    for load, store in zip(loads, stores):
        load.wait()
        store.start()
    flats = []
    for c in range(2):
        cosine = waves[2 * c * span : (2 * c + 1) * span]
        sine = waves[(2 * c + 1) * span : (2 * c + 2) * span]
        flats.append(cosine - pltpu.roll(sine, span, 1))
        flats.append(-(pltpu.roll(cosine, span, 1) + sine))
    flat = jnp.concatenate(flats, axis=0)[:, :span] * norm
    pieces = []
    for _ in range(3):
        piece = flat.astype(jnp.bfloat16)
        pieces.append(piece)
        flat = flat - piece.astype(jnp.float32)
    left_side = jnp.concatenate(pieces, axis=1)

    chunk = 512
    total = orders.shape[1]
    index = lax.broadcasted_iota(jnp.int32, (span, chunk), 0) - span // 2
    for start in range(0, total, chunk):
        at = slice(start, start + chunk)
        kx = index == orders[0:1, at]
        ky = jnp.where(index == orders[1:2, at], 1.0, 0.0).astype(jnp.bfloat16)
        picked = jnp.dot(
            left_side,
            jnp.concatenate([ky] * 3, axis=0),
            preferred_element_type=jnp.float32,
        )
        for r in range(4):
            pupil[r : r + 1, at] = jnp.sum(
                jnp.where(kx, picked[r * span : (r + 1) * span], 0.0), axis=0, keepdims=True
            )
    for store in stores:
        store.wait()


def shards(
    e_field,
    h_field,
    polar,
    current,
    psi_h,
    psi_e,
    material,
    inv_eps_table,
    decay_table,
    drive_table,
    strength_table,
    spring_table,
    orders,
):
    count = lax.axis_size("gx")
    planes, depth, cells = material.shape
    layers = psi_h.shape[2]
    f32 = jnp.float32
    rows = -(-2 * planes // ROWS) * ROWS
    ytab = jnp.asarray(wave_table(cells, KSPAN).astype(np.float32))
    xmat = jnp.asarray(x_matrix(count, planes, rows, KSPAN))
    hbm = pl.BlockSpec(memory_space=pltpu.MemorySpace.HBM)
    vmem = pl.BlockSpec(memory_space=pltpu.MemorySpace.VMEM)
    smem = pl.BlockSpec(memory_space=pltpu.MemorySpace.SMEM)
    dma = pltpu.SemaphoreType.DMA
    limit = 56 * 1024 * 1024
    turned = (planes, layers, 2, cells)
    field = e_field.shape
    shape = jax.ShapeDtypeStruct
    state = [shape(field, f32)] * 4 + [shape(turned, f32)] * 2
    lines = (count, rows, 2 * KSPAN)
    edges = (STEPS, depth // ROWS)
    outs = pl.pallas_call(
        functools.partial(step_kernel, count, layers),
        out_shape=state + [shape(lines, f32)],
        in_specs=[hbm] * 8 + [smem] * 5,
        out_specs=[hbm] * 7,
        scratch_shapes=[pltpu.VMEM(field, f32)] * 4
        + [pltpu.VMEM(turned, f32)] * 2
        + [
            pltpu.VMEM(material.shape, jnp.int32),
            pltpu.VMEM((4, ROWS, LANES), f32),
            pltpu.VMEM((4,) + material.shape, f32),
            pltpu.VMEM((2, planes, ROWS, cells), f32),
            pltpu.VMEM((2, planes, ROWS, cells), f32),
            pltpu.VMEM((STEPS, 2, depth, cells), f32),
            pltpu.VMEM((STEPS, 2, depth, cells), f32),
            pltpu.VMEM(ytab.shape, f32),
            pltpu.VMEM((rows, cells), f32),
            pltpu.VMEM(lines, f32),
            dma((8,)),
            dma((7,)),
            dma(edges),
            dma(edges),
            dma(edges),
            dma(edges),
            dma((count,)),
            dma((count,)),
        ],
        compiler_params=pltpu.CompilerParams(
            collective_id=0, has_side_effects=True, vmem_limit_bytes=limit
        ),
    )(
        e_field,
        h_field,
        polar,
        current,
        jnp.transpose(psi_h, (1, 2, 0, 3)),
        jnp.transpose(psi_e, (1, 2, 0, 3)),
        material,
        ytab,
        inv_eps_table,
        decay_table,
        drive_table,
        strength_table,
        spring_table,
    )
    copies = 4 * field[0] + 2 * planes
    results = pl.pallas_call(
        functools.partial(result_kernel, 1.0 / math.sqrt(count * planes * cells)),
        out_shape=state + [shape((4, orders.shape[1]), f32)],
        in_specs=[hbm] * 8 + [vmem],
        out_specs=[hbm] * 6 + [vmem],
        scratch_shapes=[pltpu.VMEM(field, f32)] * 4
        + [pltpu.VMEM(turned, f32)] * 2
        + [
            pltpu.VMEM(lines, f32),
            pltpu.VMEM(xmat.shape, f32),
            dma((copies,)),
            dma((copies,)),
            dma((2,)),
        ],
        compiler_params=pltpu.CompilerParams(vmem_limit_bytes=limit),
    )(*outs, xmat, orders)
    psi_h_out = jnp.transpose(results[4], (2, 0, 1, 3))
    psi_e_out = jnp.transpose(results[5], (2, 0, 1, 3))
    return (*results[:4], psi_h_out, psi_e_out, results[6])


def solution(mesh):
    field = P(None, ("mask", "gx"), None, None)
    in_specs = (field,) * 6 + (P(("mask", "gx"), None, None),) + (P(),) * 6
    out_specs = (field,) * 6 + (P(None, "mask"),)
    return jax.shard_map(shards, mesh=mesh, in_specs=in_specs, out_specs=out_specs, check_vma=False)
```

```python
import functools
import math

import jax
import jax.numpy as jnp
import numpy as np
from jax import lax
from jax.experimental import pallas as pl
from jax.experimental.pallas import tpu as pltpu
from jax.sharding import PartitionSpec as P

KSPAN = 64
STEPS = 4
COURANT = 0.5
SIGMA_MAX = 0.8
PML_ALPHA = 0.05
ROWS = 8
LANES = 128


def profile_values(layers):
    out = []
    for offset in (0.5, 0.0):
        depth = (layers - np.arange(layers, dtype=np.float64) - offset) / layers
        sigma = SIGMA_MAX * depth**3
        decay = np.exp(-(sigma + PML_ALPHA))
        gain = sigma / (sigma + PML_ALPHA) * (decay - 1.0)
        out += [decay, gain]
    return out


def wave_table(cells, span):
    rows = np.arange(cells, dtype=np.int64)
    waves = np.arange(span, dtype=np.int64) - span // 2
    phase = (rows[:, None] * waves[None, :] % cells) * (2.0 * math.pi / cells)
    return np.concatenate([np.cos(phase), np.sin(phase)], axis=1)


def x_matrix(count, planes, rows, span):
    waves = wave_table(count * planes, span).T.reshape(2 * span, count, planes)
    out = np.zeros((2, 2 * span, count, rows))
    for comp in range(2):
        out[comp, :, :, comp * planes : (comp + 1) * planes] = waves
    return out.reshape(4 * span, count * rows).astype(np.float32)


def step_kernel(
    count,
    layers,
    e_in,
    h_in,
    p_in,
    c_in,
    psi_h_in,
    psi_e_in,
    mat_in,
    ytab_in,
    xmat_in,
    inv_eps_table,
    decay_table,
    drive_table,
    strength_table,
    spring_table,
    orders,
    e_out,
    h_out,
    p_out,
    c_out,
    psi_h_out,
    psi_e_out,
    pupil_out,
    e,
    h,
    pol,
    cur,
    raw_h,
    raw_e,
    mat,
    prof,
    coefs,
    psi_h,
    psi_e,
    ahead,
    behind,
    ytab,
    line,
    gathered,
    xmat,
    pupil,
    load_sem,
    store_sem,
    left_send,
    left_recv,
    right_send,
    right_recv,
    all_send,
    all_recv,
):
    planes, depth, cells = mat.shape
    tiles = depth // ROWS
    last = planes - 1
    me = lax.axis_index("gx")
    right, left = lax.rem(me + 1, count), lax.rem(me + count - 1, count)

    loads = [
        pltpu.make_async_copy(source, target, load_sem.at[index])
        for index, (source, target) in enumerate(
            [
                (e_in, e),
                (h_in, h),
                (psi_h_in, raw_h),
                (mat_in, mat),
                (c_in, cur),
                (p_in, pol),
                (psi_e_in, raw_e),
                (ytab_in, ytab),
                (xmat_in, xmat),
            ]
        )
    ]
    for load in loads:
        load.start()
    stores = [
        pltpu.make_async_copy(source, target, store_sem.at[index])
        for index, (source, target) in enumerate(
            [
                (h, h_out),
                (e, e_out),
                (cur, c_out),
                (pol, p_out),
                (raw_h, psi_h_out),
                (raw_e, psi_e_out),
                (pupil, pupil_out),
            ]
        )
    ]

    barrier = pltpu.get_barrier_semaphore()

    def greet(k, carry):
        pl.semaphore_signal(
            barrier,
            inc=1,
            device_id={"gx": lax.rem(me + k, count)},
            device_id_type=pl.DeviceIdType.MESH,
        )
        return carry

    lax.fori_loop(1, count, greet, 0)

    level = lax.broadcasted_iota(jnp.int32, (ROWS, LANES), 0)
    for index, values in enumerate(profile_values(layers)):
        total = jnp.zeros((ROWS, LANES), jnp.float32)
        for z in range(layers):
            total = jnp.where(level == z, float(values[z]), total)
        prof[index] = total

    row = lax.broadcasted_iota(jnp.int32, (ROWS, cells), 0)
    first_row = row == 0
    last_row = row == ROWS - 1

    def wide(index):
        return jnp.concatenate([prof[index]] * (cells // LANES), axis=1)

    def rows_of(t):
        return slice(t * ROWS, (t + 1) * ROWS)

    def tile(ref, t):
        return ref[rows_of(t), :]

    def z_next(ref, t):
        moved = pltpu.roll(tile(ref, t), ROWS - 1, 0)
        if t == tiles - 1:
            return jnp.where(last_row, 0.0, moved)
        return jnp.where(last_row, ref[(t + 1) * ROWS : (t + 1) * ROWS + 1, :], moved)

    def z_prev(ref, t):
        moved = pltpu.roll(tile(ref, t), 1, 0)
        if t == 0:
            return jnp.where(first_row, 0.0, moved)
        return jnp.where(first_row, ref[t * ROWS - 1 : t * ROWS, :], moved)

    def y_next(value):
        return pltpu.roll(value, cells - 1, 1)

    def y_prev(value):
        return pltpu.roll(value, 1, 1)

    def h_tile(p, t, whole):
        at = rows_of(t)
        ex, ey = e.at[0, p], e.at[1, p]
        x, y, z = tile(ex, t), tile(ey, t), e[2, p, at, :]
        dex = z_next(ex, t) - x
        dey = z_next(ey, t) - y
        if t == 0:
            mem = wide(0) * psi_h[1, p] + wide(1) * dex
            psi_h[1, p] = mem
            dex = dex + mem
            mem = wide(0) * psi_h[0, p] + wide(1) * dey
            psi_h[0, p] = mem
            dey = dey + mem
        h[0, p, at, :] = h[0, p, at, :] - COURANT * (y_next(z) - z - dey)
        part_y = dex + z
        part_z = x - y - y_next(x)
        if whole:
            part_y = part_y - e[2, p + 1, at, :]
            part_z = part_z + e[1, p + 1, at, :]
        h[1, p, at, :] = h[1, p, at, :] - COURANT * part_y
        h[2, p, at, :] = h[2, p, at, :] - COURANT * part_z

    def e_tile(p, t, hy_b, hz_b):
        at = rows_of(t)
        hx, hy = h.at[0, p], h.at[1, p]
        x, y, z = tile(hx, t), tile(hy, t), h[2, p, at, :]
        dhy = y - z_prev(hy, t)
        dhx = x - z_prev(hx, t)
        if t == 0:
            mem = wide(2) * psi_e[0, p] + wide(3) * dhy
            psi_e[0, p] = mem
            dhy = dhy + mem
            mem = wide(2) * psi_e[1, p] + wide(3) * dhx
            psi_e[1, p] = mem
            dhx = dhx + mem
        curl = (
            z - y_prev(z) - dhy,
            dhx - (z - hz_b),
            y - hy_b - (x - y_prev(x)),
        )
        inv_eps = coefs[0, p, at, :]
        decay = coefs[1, p, at, :]
        pull = coefs[2, p, at, :]
        hold = coefs[3, p, at, :]
        for c in range(3):
            field = e[c, p, at, :]
            polar = pol[c, p, at, :]
            current = decay * cur[c, p, at, :] + (pull * field - hold * polar)
            cur[c, p, at, :] = current
            pol[c, p, at, :] = polar + current
            e[c, p, at, :] = field + inv_eps * (COURANT * curl[c] - current)

    def e_own(p, t):
        e_tile(p, t, h[1, p - 1, rows_of(t), :], h[2, p - 1, rows_of(t), :])

    def to_left(step, t):
        return pltpu.make_async_remote_copy(
            src_ref=e.at[1:3, 0, rows_of(t)],
            dst_ref=ahead.at[step, :, rows_of(t)],
            send_sem=left_send.at[step, t],
            recv_sem=left_recv.at[step, t],
            device_id={"gx": left},
            device_id_type=pl.DeviceIdType.MESH,
        )

    def to_right(step, t):
        return pltpu.make_async_remote_copy(
            src_ref=h.at[1:3, last, rows_of(t)],
            dst_ref=behind.at[step, :, rows_of(t)],
            send_sem=right_send.at[step, t],
            recv_sem=right_recv.at[step, t],
            device_id={"gx": right},
            device_id_type=pl.DeviceIdType.MESH,
        )

    def fill_psi(source, target):
        def fill(p, carry):
            for c in range(2):
                target[c, p] = jnp.zeros((ROWS, cells), jnp.float32)
                for z in range(layers):
                    target[c, p, z : z + 1, :] = source[p, z, c : c + 1, :]
            return carry

        lax.fori_loop(0, planes, fill, 0)

    def drain_psi(source, target):
        def drain(p, carry):
            for c in range(2):
                for z in range(layers):
                    target[p, z, c : c + 1, :] = source[c, p, z : z + 1, :]
            return carry

        lax.fori_loop(0, planes, drain, 0)

    for load in loads[:3]:
        load.wait()
    fill_psi(raw_h, psi_h)
    h_tile(last, 0, False)
    pl.semaphore_wait(barrier, count - 1)
    for t in range(tiles):
        to_left(0, t).start()
        if t > 0:
            h_tile(last, t, False)
        to_right(0, t).start()

    materials = inv_eps_table.shape[0]
    tables = (
        [inv_eps_table[i] for i in range(materials)],
        [decay_table[i] for i in range(materials)],
        [drive_table[i] * strength_table[i] for i in range(materials)],
        [drive_table[i] * spring_table[i] for i in range(materials)],
    )
    loads[3].wait()

    def fill_coefs(p, carry):
        for t in range(tiles):
            m = mat[p, rows_of(t), :]
            same = [m == i for i in range(materials)]
            for index, table in enumerate(tables):
                value = jnp.zeros((ROWS, cells), jnp.float32)
                for i in range(materials):
                    value = jnp.where(same[i], table[i], value)
                coefs[index, p, rows_of(t), :] = value
        return carry

    lax.fori_loop(0, planes, fill_coefs, 0)
    for load in loads[4:]:
        load.wait()
    fill_psi(raw_e, psi_e)

    def share(k):
        return pltpu.make_async_remote_copy(
            src_ref=gathered.at[me],
            dst_ref=gathered.at[me],
            send_sem=all_send.at[k],
            recv_sem=all_recv.at[me],
            device_id={"gx": lax.rem(me + k, count)},
            device_id_type=pl.DeviceIdType.MESH,
        )

    def start_share(k, carry):
        share(k).start()
        return carry

    def transform():
        line[...] = jnp.zeros(line.shape, jnp.float32)
        for c in range(2):
            for p in range(planes):
                line[c * planes + p : c * planes + p + 1, :] = e[c, p, layers : layers + 1, :]
        gathered[me] = jnp.dot(
            line[...],
            ytab[...],
            precision=lax.Precision.HIGHEST,
            preferred_element_type=jnp.float32,
        )
        lax.fori_loop(1, count, start_share, 0)

    def run_step(step, carry):
        def h_inner(p, c):
            for t in range(tiles):
                h_tile(p, t, True)
            return c

        lax.fori_loop(0, last, h_inner, 0)
        more = step < STEPS - 1

        def next_right(t):
            h_tile(last, t, False)
            to_right(step + 1, t).start()

        def e_first(p, c):
            e_own(p, 0)
            return c

        for t in range(tiles):
            if t == 1:
                lax.fori_loop(1, last, e_first, 0)

                @pl.when(jnp.logical_not(more))
                def _():
                    transform()

            at = rows_of(t)
            to_left(step, t).wait()
            to_right(step, t).wait()
            h[1, last, at, :] = h[1, last, at, :] + COURANT * ahead[step, 1, at, :]
            h[2, last, at, :] = h[2, last, at, :] - COURANT * ahead[step, 0, at, :]
            hy_b = behind[step, 0, at, :] + COURANT * e[2, 0, at, :]
            hz_b = behind[step, 1, at, :] - COURANT * e[1, 0, at, :]
            e_tile(0, t, hy_b, hz_b)

            @pl.when(more)
            def _():
                to_left(step + 1, t).start()

            e_own(last, t)

            @pl.when(more)
            def _():
                if t > 0:
                    next_right(t - 1)
                if t == tiles - 1:
                    next_right(t)

        @pl.when(jnp.logical_not(more))
        def _():
            stores[0].start()

        def e_inner(p, c):
            for t in range(1, tiles):
                e_own(p, t)
            return c

        lax.fori_loop(1, last, e_inner, 0)
        return carry

    lax.fori_loop(0, STEPS, run_step, 0)

    for store in stores[1:4]:
        store.start()
    drain_psi(psi_h, raw_h)
    stores[4].start()
    drain_psi(psi_e, raw_e)
    stores[5].start()

    def end_share(k, carry):
        other = lax.rem(me + k, count)
        pltpu.make_async_remote_copy(
            src_ref=gathered.at[other],
            dst_ref=gathered.at[other],
            send_sem=all_send.at[k],
            recv_sem=all_recv.at[other],
            device_id={"gx": other},
            device_id_type=pl.DeviceIdType.MESH,
        ).wait_recv()
        return carry

    def end_send(k, carry):
        share(k).wait_send()
        return carry

    lax.fori_loop(1, count, end_share, 0)
    lax.fori_loop(1, count, end_send, 0)

    span = KSPAN
    waves = jnp.dot(
        xmat[...],
        gathered[...].reshape(gathered.shape[0] * gathered.shape[1], 2 * span),
        precision=lax.Precision.HIGHEST,
        preferred_element_type=jnp.float32,
    )
    flats = []
    for c in range(2):
        cosine = waves[2 * c * span : (2 * c + 1) * span]
        sine = waves[(2 * c + 1) * span : (2 * c + 2) * span]
        flats.append(cosine - pltpu.roll(sine, span, 1))
        flats.append(-(pltpu.roll(cosine, span, 1) + sine))
    flat = jnp.concatenate(flats, axis=0)[:, :span] * (1.0 / math.sqrt(count * planes * cells))
    pieces = []
    for _ in range(3):
        piece = flat.astype(jnp.bfloat16)
        pieces.append(piece)
        flat = flat - piece.astype(jnp.float32)
    left_side = jnp.concatenate(pieces, axis=1)

    chunk = 512
    total = orders.shape[1]
    index = lax.broadcasted_iota(jnp.int32, (span, chunk), 0) - span // 2
    for start in range(0, total, chunk):
        at = slice(start, start + chunk)
        kx = index == orders[0:1, at]
        ky = jnp.where(index == orders[1:2, at], 1.0, 0.0).astype(jnp.bfloat16)
        picked = jnp.dot(
            left_side,
            jnp.concatenate([ky] * 3, axis=0),
            preferred_element_type=jnp.float32,
        )
        for r in range(4):
            pupil[r : r + 1, at] = jnp.sum(
                jnp.where(kx, picked[r * span : (r + 1) * span], 0.0), axis=0, keepdims=True
            )
    stores[6].start()
    for store in stores:
        store.wait()


def result_kernel(*refs):
    ins, outs, held, (in_sem, out_sem) = refs[:7], refs[7:14], refs[14:21], refs[21:]
    loads, stores = [], []
    for source, target, buffer in zip(ins, outs, held):
        pieces = [slice(None)] if len(buffer.shape) == 2 else range(buffer.shape[0])
        for piece in pieces:
            sem = len(loads)
            loads.append(
                pltpu.make_async_copy(source.at[piece], buffer.at[piece], in_sem.at[sem])
            )
            stores.append(
                pltpu.make_async_copy(buffer.at[piece], target.at[piece], out_sem.at[sem])
            )
    for load in loads:
        load.start()
    for load, store in zip(loads, stores):
        load.wait()
        store.start()
    for store in stores:
        store.wait()


def shards(
    e_field,
    h_field,
    polar,
    current,
    psi_h,
    psi_e,
    material,
    inv_eps_table,
    decay_table,
    drive_table,
    strength_table,
    spring_table,
    orders,
):
    count = lax.axis_size("gx")
    planes, depth, cells = material.shape
    layers = psi_h.shape[2]
    f32 = jnp.float32
    rows = -(-2 * planes // ROWS) * ROWS
    ytab = jnp.asarray(wave_table(cells, KSPAN).astype(np.float32))
    xmat = jnp.asarray(x_matrix(count, planes, rows, KSPAN))
    hbm = pl.BlockSpec(memory_space=pltpu.MemorySpace.HBM)
    vmem = pl.BlockSpec(memory_space=pltpu.MemorySpace.VMEM)
    smem = pl.BlockSpec(memory_space=pltpu.MemorySpace.SMEM)
    dma = pltpu.SemaphoreType.DMA
    limit = 56 * 1024 * 1024
    turned = (planes, layers, 2, cells)
    field = e_field.shape
    shape = jax.ShapeDtypeStruct
    found = (4, orders.shape[1])
    state = [shape(field, f32)] * 4 + [shape(turned, f32)] * 2 + [shape(found, f32)]
    lines = (count, rows, 2 * KSPAN)
    edges = (STEPS, depth // ROWS)
    outs = pl.pallas_call(
        functools.partial(step_kernel, count, layers),
        out_shape=state,
        in_specs=[hbm] * 9 + [smem] * 5 + [vmem],
        out_specs=[hbm] * 7,
        scratch_shapes=[pltpu.VMEM(field, f32)] * 4
        + [pltpu.VMEM(turned, f32)] * 2
        + [
            pltpu.VMEM(material.shape, jnp.int32),
            pltpu.VMEM((4, ROWS, LANES), f32),
            pltpu.VMEM((4,) + material.shape, f32),
            pltpu.VMEM((2, planes, ROWS, cells), f32),
            pltpu.VMEM((2, planes, ROWS, cells), f32),
            pltpu.VMEM((STEPS, 2, depth, cells), f32),
            pltpu.VMEM((STEPS, 2, depth, cells), f32),
            pltpu.VMEM(ytab.shape, f32),
            pltpu.VMEM((rows, cells), f32),
            pltpu.VMEM(lines, f32),
            pltpu.VMEM(xmat.shape, f32),
            pltpu.VMEM(found, f32),
            dma((9,)),
            dma((7,)),
            dma(edges),
            dma(edges),
            dma(edges),
            dma(edges),
            dma((count,)),
            dma((count,)),
        ],
        compiler_params=pltpu.CompilerParams(
            collective_id=0, has_side_effects=True, vmem_limit_bytes=limit
        ),
    )(
        e_field,
        h_field,
        polar,
        current,
        jnp.transpose(psi_h, (1, 2, 0, 3)),
        jnp.transpose(psi_e, (1, 2, 0, 3)),
        material,
        ytab,
        xmat,
        inv_eps_table,
        decay_table,
        drive_table,
        strength_table,
        spring_table,
        orders,
    )
    copies = 4 * field[0] + 2 * planes + 1
    results = pl.pallas_call(
        result_kernel,
        out_shape=state,
        in_specs=[hbm] * 7,
        out_specs=[hbm] * 7,
        scratch_shapes=[pltpu.VMEM(field, f32)] * 4
        + [pltpu.VMEM(turned, f32)] * 2
        + [pltpu.VMEM(found, f32), dma((copies,)), dma((copies,))],
        compiler_params=pltpu.CompilerParams(vmem_limit_bytes=limit),
    )(*outs)
    psi_h_out = jnp.transpose(results[4], (2, 0, 1, 3))
    psi_e_out = jnp.transpose(results[5], (2, 0, 1, 3))
    return (*results[:4], psi_h_out, psi_e_out, results[6])


def solution(mesh):
    field = P(None, ("mask", "gx"), None, None)
    in_specs = (field,) * 6 + (P(("mask", "gx"), None, None),) + (P(),) * 6
    out_specs = (field,) * 6 + (P(None, "mask"),)
    return jax.shard_map(shards, mesh=mesh, in_specs=in_specs, out_specs=out_specs, check_vma=False)
```
